32 devices in a mesh: mesh: 8 (over z, y), param: 4 (over x, core).
Axes of the slice: x: 2, y: 2, z: 4, core: 2. Of those that a mesh axis runs over, the one named last changes fastest.
Arguments:
- snapshots: bfloat16 [32768, 512], P('mesh', 'param'), may hold values from -4 to 4
- coupling: bfloat16 [256, 3, 128, 128], P('mesh'), may hold values from -0.3125 to 0.3125
- reaction_rate: float32 [512], P('param'), may hold values from 0.1 to 1
- sketch: bfloat16 [256, 128], replicated, may hold values from -0.375 to 0.375
Outputs:
- mode_basis: bfloat16 [32768, 128], P('mesh', 'param')
The draws below stay inside these ranges and needn't reach their ends.
All inputs are finite; a program needn't handle non-finite values.
Results may differ from the reference program's by a relative error of at most 0.0095.
Values may be sent and summed in bfloat16 or wider, within the bound.
A program may use at most 64 MiB of HBM per device.

```python
import math
import jax
import jax.numpy as jnp
from jax import lax

BLOCK = 128
MODES = 128
SECTIONS = 3
NBLK = 256
ROWS = 32768
TRAJ = 512
LEVELS = 2
N_PARAM = 4


def steps_of(rng, shape, pieces, least, top_value):
    def one(position, shards_of):
        steps = jax.random.uniform(jax.random.fold_in(jax.random.fold_in(rng, 6), position), (shards_of,), jnp.float32, least / len(pieces), top_value / len(pieces))
        return jnp.repeat(jnp.exp(steps), shape[position] // shards_of).reshape((-1,) + (1,) * (len(shape) - position - 1))

    level = one(*pieces[0])
    for cut in pieces[1:]:
        level = level * one(*cut)
    return level


def bell_draw(stream_key, shape, deviation, most, pieces=(), kind=jnp.bfloat16):
    loudness = steps_of(stream_key, shape, pieces, -0.22, 0.18) if pieces else 1.0
    result = jax.random.normal(stream_key, shape, jnp.float32) * deviation * loudness
    return jnp.minimum(jnp.maximum(result, -most), most).astype(kind)


def setup_inputs(seed: int = 0) -> dict:
    key_list = jax.random.split(jax.random.key(seed), 5)
    return {
        "snapshots": bell_draw(key_list[0], (ROWS, TRAJ), 1.0, 4.0, ((0, 8), (1, 4))),
        "coupling": bell_draw(key_list[1], (NBLK, 3, BLOCK, BLOCK), (3 * BLOCK) ** -0.5, 0.3125, ((0, 8),)),
        "reaction_rate": jnp.clip(jnp.exp(math.log(1.0) - 2.3025851 * jax.random.uniform(key_list[2], (TRAJ,), jnp.float32) ** steps_of(key_list[2], (TRAJ,), ((0, 4),), -0.2, 0.2)), 0.1, 1.0),
        "sketch": bell_draw(key_list[3], (2 * MODES, MODES), (2 * MODES) ** -0.5, 0.375),
    }


def run_sections(state, coupling, rate_row):
    block_count = state.shape[0] // BLOCK
    coupling_wide = coupling.astype(jnp.float32)
    for section_index in range(SECTIONS):
        current = state.astype(jnp.float32)
        blocks = current.reshape(block_count, BLOCK, MODES)
        zero_block = jnp.zeros((1, BLOCK, MODES), jnp.float32)
        below_blocks = jnp.concatenate([zero_block, blocks[:-1]], 0)
        above_blocks = jnp.concatenate([blocks[1:], zero_block], 0)
        stacked = jnp.stack([blocks, below_blocks, above_blocks], 1)
        mixed_rows = jnp.einsum('bkij,bkjm->bim', coupling_wide, stacked).reshape(state.shape)
        state = ((0.5 * current + 0.5 * mixed_rows) / (1.0 + rate_row[None, :] * current * current)).astype(jnp.bfloat16)
    return state

def scaled_inverse(gram_matrix):
    cholesky_lower = jnp.linalg.cholesky(gram_matrix)
    identity_matrix = jnp.eye(gram_matrix.shape[0], dtype=gram_matrix.dtype)
    inverse = jax.scipy.linalg.solve_triangular(cholesky_lower, identity_matrix, lower=True)
    return inverse.T * jnp.diagonal(cholesky_lower)[None, :]

def leaf_basis(state):
    gram_matrix = jnp.dot(state.T.astype(jnp.float32), state.astype(jnp.float32), preferred_element_type=jnp.float32)
    leaf_factor = scaled_inverse(gram_matrix).astype(jnp.bfloat16)
    return jnp.dot(state.astype(jnp.float32), leaf_factor.astype(jnp.float32), preferred_element_type=jnp.float32).astype(jnp.bfloat16)

def merge_pair(lower_basis, upper_basis, sketch):
    joined = jnp.concatenate([lower_basis, upper_basis], 1)
    merged = jnp.dot(joined.astype(jnp.float32), sketch.astype(jnp.float32), preferred_element_type=jnp.float32)
    gram_matrix = jnp.dot(merged.T, merged, precision=lax.Precision.HIGHEST)
    factor = scaled_inverse(gram_matrix)
    return jnp.dot(merged, factor, precision=lax.Precision.HIGHEST).astype(jnp.bfloat16)

def reference(snapshots, coupling, reaction_rate, sketch):
    total_rows = snapshots.shape[0]
    group_stack = snapshots.reshape(total_rows, N_PARAM, MODES).transpose(1, 0, 2)
    rate_rows = reaction_rate.reshape(N_PARAM, MODES)

    def one_group(items):
        return leaf_basis(run_sections(items[0], coupling, items[1]))
    bases = lax.map(one_group, (group_stack, rate_rows))

    def one_pair(pair_item):
        return merge_pair(pair_item[0], pair_item[1], sketch)
    for tree_level in range(LEVELS):
        pair_stack = bases.reshape(-1, 2, total_rows, MODES)
        bases = lax.map(one_pair, pair_stack)
    return bases[0]
```

```python
import functools

import jax
import jax.numpy as jnp
from jax import lax
from jax.experimental import pallas as pl
from jax.experimental.pallas import tpu as pltpu
from jax.sharding import PartitionSpec as P

SECTIONS = 3
MESH = pl.DeviceIdType.MESH
F32 = jnp.float32
BF16 = jnp.bfloat16


def split_two(x):
    high = x.astype(BF16)
    return high, (x - high.astype(F32)).astype(BF16)


def unit_inverse(gram):
    size = gram.shape[0]
    count = size // 8
    rows = [gram[8 * q : 8 * q + 8, :] for q in range(count)]
    lane = lax.broadcasted_iota(jnp.int32, (8, size), 1)
    sub = lax.broadcasted_iota(jnp.int32, (8, size), 0)
    for p in range(count):
        first = 8 * p
        inside = (lane >= first) & (lane < first + 8)
        columns = [
            [jnp.broadcast_to(rows[q][:, first + j : first + j + 1], (8, size)) for j in range(8)]
            for q in range(p, count)
        ]
        work = [jnp.where(inside, jnp.where(lane - first == sub, 1.0, 0.0), rows[p])]
        work += [jnp.where(inside, 0.0, rows[q]) for q in range(p + 1, count)]
        for i in range(8):
            pivot_row = jnp.broadcast_to(work[0][i : i + 1, :], (8, size))
            entries = [jnp.broadcast_to(columns[0][j][i : i + 1, :], (8, size)) for j in range(i, 8)]
            inverse = 1.0 / entries[0]
            for q in range(count - p):
                scale = columns[q][i] * inverse
                if q == 0:
                    scale = jnp.where(sub > i, scale, 0.0)
                work[q] = work[q] - scale * pivot_row
                for j in range(i + 1, 8):
                    columns[q][j] = columns[q][j] - scale * entries[j - i]
        rows[p:] = work
    full = jnp.concatenate(rows, 0)
    row = lax.broadcasted_iota(jnp.int32, (size, size), 0)
    column = lax.broadcasted_iota(jnp.int32, (size, size), 1)
    return jnp.where(column <= row, full, 0.0)


def cross(a, b):
    return lax.dot_general(a, b, (((0,), (0,)), ((), ())), preferred_element_type=F32)


def dot(a, b):
    return jnp.dot(a, b, preferred_element_type=F32)


def wait_bytes(ref, sem):
    pltpu.make_async_copy(ref, ref, sem).wait()


def kernel(plan, snap_ref, coup_ref, rate_ref, sketch_ref, out_ref, *scratch):
    n_mesh, n_param, levels, pieces = plan
    scratch = list(scratch)
    take = lambda k: [scratch.pop(0) for _ in range(k)]
    coup, packed, landed, tall = take(4)
    states = take(SECTIONS + 1)
    bases = take(levels)
    partner_rows = take(levels)
    halves = take(levels)
    partial = take(levels + 1)
    slots = take(levels + 1)
    grams = take(levels + 1)
    load_sem, halo_send, halo_recv, merge_send, merge_recv, sum_send, sum_recv, all_send, all_recv, out_send, out_recv = take(11)

    m = lax.axis_index("mesh")
    p = lax.axis_index("param")
    total_rows, modes = snap_ref.shape
    block_count, _, block, _ = coup_ref.shape

    load_state = pltpu.make_async_copy(snap_ref, states[0].at[pl.ds(block, total_rows)], load_sem.at[0])
    load_coup = pltpu.make_async_copy(coup_ref, coup, load_sem.at[1])
    load_state.start()
    load_coup.start()

    n_all = n_mesh * n_param
    me = m * n_param + p
    barrier = pltpu.get_barrier_semaphore()

    def greet(s, carry):
        t = lax.rem(me + s, n_all)
        pl.semaphore_signal(barrier, inc=1, device_id=(t // n_param, lax.rem(t, n_param)), device_id_type=MESH)
        return carry

    lax.fori_loop(1, n_all, greet, 0)
    for k in range(SECTIONS):
        @pl.when(m == 0)
        def _():
            states[k][pl.ds(0, block), :] = jnp.zeros((block, modes), BF16)

        @pl.when(m == n_mesh - 1)
        def _():
            states[k][pl.ds(block + total_rows, block), :] = jnp.zeros((block, modes), BF16)
    load_state.wait()
    pl.semaphore_wait(barrier, n_all - 1)

    def halo_up(k):
        return pltpu.make_async_remote_copy(
            states[k].at[pl.ds(total_rows, block)], states[k].at[pl.ds(0, block)],
            halo_send.at[2 * k], halo_recv.at[2 * k], device_id=(m + 1, p), device_id_type=MESH)

    def halo_down(k):
        return pltpu.make_async_remote_copy(
            states[k].at[pl.ds(block, block)], states[k].at[pl.ds(block + total_rows, block)],
            halo_send.at[2 * k + 1], halo_recv.at[2 * k + 1], device_id=(m - 1, p), device_id_type=MESH)

    def halo_start(k):
        @pl.when(m < n_mesh - 1)
        def _():
            halo_up(k).start()

        @pl.when(m > 0)
        def _():
            halo_down(k).start()

    halo_start(0)
    load_coup.wait()
    rate = rate_ref[...]

    def advance(k, b):
        c = coup.at[b]
        operator = jnp.concatenate([c[1], c[0], c[2]], 1)
        start = pl.multiple_of(b * block, block)
        mixed = dot(operator, states[k][pl.ds(start, 3 * block), :])
        at = pl.ds(pl.multiple_of(start + block, block), block)
        current = states[k][at, :].astype(F32)
        states[k + 1][at, :] = ((0.5 * current + 0.5 * mixed) / (1.0 + rate * current * current)).astype(BF16)

    inner = block_count - 2
    group = max(g for g in range(1, 11) if inner % g == 0)
    for k in range(SECTIONS):
        def some(i, carry, k=k):
            for j in range(group):
                advance(k, 1 + i * group + j)
            return carry

        lax.fori_loop(0, inner // group, some, 0)

        @pl.when(m > 0)
        def _():
            halo_up(k).wait_recv()

        @pl.when(m < n_mesh - 1)
        def _():
            halo_down(k).wait_recv()

        advance(k, 0)
        advance(k, block_count - 1)
        if k + 1 < SECTIONS:
            halo_start(k + 1)
    state = states[SECTIONS]

    def sum_over(level):
        width = 2**level
        n = n_mesh * width
        count = min(n, pieces)
        depth = modes // count
        base = p // width * width
        rank = m * width + (p - base)

        def device(t):
            return (t // width, base + lax.rem(t, width))

        def scatter(s, carry):
            t = lax.rem(rank + s, n)
            at = pl.ds(pl.multiple_of(lax.rem(t, count) * depth, depth), depth)
            pltpu.make_async_remote_copy(
                partial[level].at[at], slots[level].at[s - 1], sum_send.at[level], sum_recv.at[level],
                device_id=device(t), device_id_type=MESH).start()
            return carry

        lax.fori_loop(1, n, scatter, 0)
        piece = lax.rem(rank, count)
        own = pl.ds(pl.multiple_of(piece * depth, depth), depth)
        wait_bytes(slots[level], sum_recv.at[level])
        if n <= 64:
            total = partial[level][own, :] + jnp.sum(slots[level][...], 0)
        else:
            total = partial[level][own, :] + lax.fori_loop(
                0, n - 1, lambda i, a: a + slots[level][i], jnp.zeros((depth, modes), F32))
        grams[level][own, :] = total

        def spread(s, carry):
            t = rank - piece + lax.rem(piece + s, count)
            pltpu.make_async_remote_copy(
                grams[level].at[own], grams[level].at[own], all_send.at[level], all_recv.at[level],
                device_id=device(t), device_id_type=MESH).start()
            return carry

        lax.fori_loop(1, count, spread, 0)
        wait_bytes(grams[level].at[pl.ds(0, (count - 1) * depth)], all_recv.at[level])
        return grams[level][...]

    chunk = 512
    gram = jnp.zeros((modes, modes), F32)
    for i in range(total_rows // chunk):
        part = state[pl.ds(block + i * chunk, chunk), :]
        gram += cross(part, part)
    partial[0][...] = gram
    factor = unit_inverse(sum_over(0)).T.astype(BF16)

    def merge_copy(level):
        held = total_rows // 2**level
        keep = p // 2**level % 2
        away = pl.ds(pl.multiple_of((1 - keep) * (held // 2), 16), held // 2)
        return pltpu.make_async_remote_copy(
            bases[level].at[away], partner_rows[level], merge_send.at[level], merge_recv.at[level],
            device_id=(m, p + (1 - 2 * keep) * 2**level), device_id_type=MESH)

    for level in range(levels):
        held = total_rows // 2**level
        half = held // 2
        keep = p // 2**level % 2
        step = min(half, chunk)
        for side in range(2):
            first = (1 - keep if side == 0 else keep) * half
            for i in range(half // step):
                at = pl.multiple_of(first + i * step, 16)
                if level == 0:
                    basis = dot(state[pl.ds(pl.multiple_of(at + block, 16), step), :], factor)
                else:
                    pair = halves[level - 1][pl.ds(at, step), :]
                    basis = dot(pair, twice) + dot(pair[:, :modes], rest)
                bases[level][pl.ds(at, step), :] = basis.astype(BF16)
            if side == 0:
                merge_copy(level).start()
        mine = sketch_ref[pl.ds(pl.multiple_of(keep * modes, modes), modes), :]
        theirs = sketch_ref[pl.ds(pl.multiple_of((1 - keep) * modes, modes), modes), :]
        weights = jnp.concatenate([mine, theirs], 0)
        merge_copy(level).wait_recv()
        gram = jnp.zeros((modes, 2 * modes), F32)
        for i in range(half // step):
            own = bases[level][pl.ds(pl.multiple_of(keep * half + i * step, 16), step), :]
            other = partner_rows[level][pl.ds(i * step, step), :]
            high, low = split_two(dot(jnp.concatenate([own, other], 1), weights))
            pair = jnp.concatenate([high, low], 1)
            halves[level][pl.ds(i * step, step), :] = pair
            gram += cross(high, pair)
        partial[level + 1][...] = gram[:, :modes] + gram[:, modes:] + gram[:, modes:].T
        high, rest = split_two(unit_inverse(sum_over(level + 1)).T)
        twice = jnp.concatenate([high, high], 0)

    share = modes // n_param
    rows = total_rows // n_param
    cut = rows // n_param
    for i in range(n_param):
        pair = halves[levels - 1][pl.ds(i * cut, cut), :]
        tall[pl.ds(i * cut, cut), :] = dot(pair, twice) + dot(pair[:, :modes], rest)
    lane = lax.broadcasted_iota(jnp.int32, (cut, modes), 1) // share
    for q in range(n_param):
        value = jnp.zeros((cut, modes), F32)
        for a in range(n_param):
            turned = tall[pl.ds(a * cut, cut), :]
            if a != q:
                turned = pltpu.roll(turned, (a - q) % n_param * share, 1)
            value = jnp.where(lane == a, turned, value)
        packed[q] = value.astype(BF16)

    def deliver(s, carry):
        t = lax.rem(p + s, n_param)
        pltpu.make_async_remote_copy(
            packed.at[t], landed.at[s - 1], out_send.at[0], out_recv.at[0],
            device_id=(m, t), device_id_type=MESH).start()
        return carry

    lax.fori_loop(1, n_param, deliver, 0)

    def unpack(source, value):
        start = 0
        for level in range(levels):
            start = start + source // 2**level % 2 * (total_rows // 2 ** (level + 1))
        for a in range(n_param):
            turned = value if a == 0 else pltpu.roll(value, (n_param - a) * share, 1)
            out_ref[pl.ds(pl.multiple_of(start + a * cut, 16), cut), :] = turned[:, :share].astype(BF16)

    unpack(p, packed[p].astype(F32))
    wait_bytes(landed, out_recv.at[0])
    for s in range(1, n_param):
        unpack(lax.rem(p + n_param - s, n_param), landed[s - 1].astype(F32))

    for k in range(SECTIONS):
        @pl.when(m < n_mesh - 1)
        def _():
            halo_up(k).wait_send()

        @pl.when(m > 0)
        def _():
            halo_down(k).wait_send()
    for level in range(levels):
        merge_copy(level).wait_send()
    for level in range(levels + 1):
        count = min(n_mesh * 2**level, pieces)
        wait_bytes(slots[level], sum_send.at[level])
        wait_bytes(grams[level].at[pl.ds(0, (count - 1) * (modes // count))], all_send.at[level])
    wait_bytes(landed, out_send.at[0])


def solution(mesh):
    n_mesh, n_param = mesh.shape["mesh"], mesh.shape["param"]
    levels = n_param.bit_length() - 1

    def on_device(snapshots, coupling, reaction_rate, sketch):
        rows, modes = snapshots.shape
        block = coupling.shape[2]
        pieces = modes // 8
        square = pltpu.VMEM((modes, modes), F32)
        slots = []
        for level in range(levels + 1):
            n = n_mesh * 2**level
            slots.append(pltpu.VMEM((n - 1, modes // min(n, pieces), modes), F32))
        cut = rows // n_param // n_param
        dma = lambda k: pltpu.SemaphoreType.DMA((k,))
        scratch = [
            pltpu.VMEM(coupling.shape, BF16),
            pltpu.VMEM((n_param, cut, modes), BF16),
            pltpu.VMEM((n_param - 1, cut, modes), BF16),
            pltpu.VMEM((rows // n_param, modes), F32),
        ]
        scratch += [pltpu.VMEM((rows + 2 * block, modes), BF16)] * (SECTIONS + 1)
        scratch += [pltpu.VMEM((rows >> k, modes), BF16) for k in range(levels)]
        scratch += [pltpu.VMEM((rows >> (k + 1), modes), BF16) for k in range(levels)]
        scratch += [pltpu.VMEM((rows >> (k + 1), 2 * modes), BF16) for k in range(levels)]
        scratch += [square] * (levels + 1) + slots + [square] * (levels + 1)
        scratch += [dma(2), dma(2 * SECTIONS), dma(2 * SECTIONS), dma(levels), dma(levels)]
        scratch += [dma(levels + 1)] * 4 + [dma(1), dma(1)]
        vmem = pl.BlockSpec(memory_space=pltpu.VMEM)
        anywhere = pl.BlockSpec(memory_space=pl.ANY)
        return pl.pallas_call(
            functools.partial(kernel, (n_mesh, n_param, levels, pieces)),
            out_shape=jax.ShapeDtypeStruct((rows, modes // n_param), BF16),
            in_specs=[anywhere, anywhere, vmem, vmem],
            out_specs=vmem,
            scratch_shapes=scratch,
            compiler_params=pltpu.CompilerParams(
                collective_id=0, has_side_effects=True, vmem_limit_bytes=48 * 1024 * 1024
            ),
        )(snapshots, coupling, reaction_rate.reshape(1, modes), sketch)

    return jax.shard_map(
        on_device,
        mesh=mesh,
        in_specs=(P("mesh", "param"), P("mesh", None, None, None), P("param"), P()),
        out_specs=P("mesh", "param"),
        check_vma=False,
    )
```

```python
import functools

import jax
import jax.numpy as jnp
from jax import lax
from jax.experimental import pallas as pl
from jax.experimental.pallas import tpu as pltpu
from jax.sharding import PartitionSpec as P

SECTIONS = 3
MESH = pl.DeviceIdType.MESH
F32 = jnp.float32
BF16 = jnp.bfloat16


def split_two(x):
    high = x.astype(BF16)
    return high, (x - high.astype(F32)).astype(BF16)


def reciprocal(x):
    guess = pl.reciprocal(x, approx=True)
    guess = guess * (2.0 - x * guess)
    return guess * (2.0 - x * guess)


def unit_inverse(gram):
    size = gram.shape[0]
    count = size // 8
    tile = (8, size)
    rows = [gram[8 * q : 8 * q + 8, :] for q in range(count)]
    lane = lax.broadcasted_iota(jnp.int32, tile, 1)
    sub = lax.broadcasted_iota(jnp.int32, tile, 0)

    def stacked(parts):
        whole = parts[7]
        for i in range(7):
            whole = jnp.where(sub == i, parts[i], whole)
        return whole

    for p in range(count):
        first = 8 * p
        inside = (lane >= first) & (lane < first + 8)
        corner = [jnp.broadcast_to(rows[p][:, first + j : first + j + 1], tile) for j in range(8)]
        entry = [[jnp.broadcast_to(corner[j][i : i + 1, :], tile) if j >= i else None for j in range(8)] for i in range(8)]
        start = jnp.where(inside, jnp.where(lane - first == sub, 1.0, 0.0), rows[p])
        line = [jnp.broadcast_to(start[i : i + 1, :], tile) for i in range(8)]
        later = [None] * (p + 1) + [jnp.where(inside, 0.0, rows[q]) for q in range(p + 1, count)]
        if p + 1 < count:
            column = [jnp.broadcast_to(rows[p + 1][:, first + j : first + j + 1], tile) for j in range(8)]
        inverse = []
        for i in range(8):
            inverse.append(reciprocal(entry[i][i]))
            for r in range(i + 1, 8):
                scale = entry[i][r] * inverse[i]
                for j in range(r, 8):
                    entry[r][j] = entry[r][j] - scale * entry[i][j]
                line[r] = line[r] - scale * line[i]
            if p + 1 < count:
                scale = column[i] * inverse[i]
                for j in range(i + 1, 8):
                    column[j] = column[j] - scale * entry[i][j]
                later[p + 1] = later[p + 1] - scale * line[i]
        if p + 2 < count:
            turned = stacked([line[i] * inverse[i] for i in range(8)]).T
            for q in range(p + 2, count):
                scales = turned[8 * q : 8 * q + 8, :]
                for i in range(8):
                    later[q] = later[q] - jnp.broadcast_to(scales[:, i : i + 1], tile) * line[i]
        rows[p] = stacked(line)
        rows[p + 1 :] = later[p + 1 :]
    full = jnp.concatenate(rows, 0)
    row = lax.broadcasted_iota(jnp.int32, (size, size), 0)
    column = lax.broadcasted_iota(jnp.int32, (size, size), 1)
    return jnp.where(column <= row, full, 0.0)


def cross(a, b):
    return lax.dot_general(a, b, (((0,), (0,)), ((), ())), preferred_element_type=F32)


def dot(a, b):
    return jnp.dot(a, b, preferred_element_type=F32)


def dot_turned(a, b):
    return lax.dot_general(a, b, (((1,), (1,)), ((), ())), preferred_element_type=F32)


def wait_bytes(ref, sem):
    pltpu.make_async_copy(ref, ref, sem).wait()


def kernel(plan, snap_ref, coup_ref, rate_hbm, sketch_hbm, out_ref, *scratch):
    n_mesh, n_param, levels, pieces = plan
    scratch = list(scratch)
    take = lambda k: [scratch.pop(0) for _ in range(k)]
    coup, rate_ref, sketch_ref, turned, result = take(5)
    states = take(SECTIONS + 1)
    partner_rows = take(levels)
    factors = take(levels)
    partner_factors = take(levels)
    halves = take(levels)
    partial = take(levels + 1)
    slots = take(levels + 1)
    grams = take(levels + 1)
    load_sem, halo_send, halo_recv, merge_send, merge_recv, factor_send, factor_recv, sum_send, sum_recv, all_send, all_recv, out_send, out_recv = take(13)

    m = lax.axis_index("mesh")
    p = lax.axis_index("param")
    total_rows, modes = snap_ref.shape
    block_count, _, block, _ = coup_ref.shape

    load_state = pltpu.make_async_copy(snap_ref, states[0].at[pl.ds(block, total_rows)], load_sem.at[0])
    load_coup = pltpu.make_async_copy(coup_ref, coup, load_sem.at[1])
    load_rate = pltpu.make_async_copy(rate_hbm, rate_ref, load_sem.at[2])
    load_sketch = pltpu.make_async_copy(sketch_hbm, sketch_ref, load_sem.at[3])
    load_state.start()
    load_coup.start()
    load_rate.start()
    load_sketch.start()

    n_all = n_mesh * n_param
    me = m * n_param + p
    barrier = pltpu.get_barrier_semaphore()

    def greet(s, carry):
        t = lax.rem(me + s, n_all)
        pl.semaphore_signal(barrier, inc=1, device_id=(t // n_param, lax.rem(t, n_param)), device_id_type=MESH)
        return carry

    lax.fori_loop(1, n_all, greet, 0)
    for k in range(SECTIONS):
        @pl.when(m == 0)
        def _():
            states[k][pl.ds(0, block), :] = jnp.zeros((block, modes), BF16)

        @pl.when(m == n_mesh - 1)
        def _():
            states[k][pl.ds(block + total_rows, block), :] = jnp.zeros((block, modes), BF16)
    load_state.wait()
    pl.semaphore_wait(barrier, n_all - 1)

    def halo_up(k):
        return pltpu.make_async_remote_copy(
            states[k].at[pl.ds(total_rows, block)], states[k].at[pl.ds(0, block)],
            halo_send.at[2 * k], halo_recv.at[2 * k], device_id=(m + 1, p), device_id_type=MESH)

    def halo_down(k):
        return pltpu.make_async_remote_copy(
            states[k].at[pl.ds(block, block)], states[k].at[pl.ds(block + total_rows, block)],
            halo_send.at[2 * k + 1], halo_recv.at[2 * k + 1], device_id=(m - 1, p), device_id_type=MESH)

    def halo_start(k):
        @pl.when(m < n_mesh - 1)
        def _():
            halo_up(k).start()

        @pl.when(m > 0)
        def _():
            halo_down(k).start()

    halo_start(0)
    load_rate.wait()
    load_sketch.wait()
    load_coup.wait()
    rate = rate_ref[...]

    def advance(k, b):
        c = coup.at[b]
        operator = jnp.concatenate([c[1], c[0], c[2]], 1)
        start = pl.multiple_of(b * block, block)
        mixed = dot(operator, states[k][pl.ds(start, 3 * block), :])
        at = pl.ds(pl.multiple_of(start + block, block), block)
        current = states[k][at, :].astype(F32)
        states[k + 1][at, :] = ((0.5 * current + 0.5 * mixed) / (1.0 + rate * current * current)).astype(BF16)

    inner = block_count - 2
    group = max(g for g in range(1, 11) if inner % g == 0)
    for k in range(SECTIONS):
        def some(i, carry, k=k):
            for j in range(group):
                advance(k, 1 + i * group + j)
            return carry

        lax.fori_loop(0, inner // group, some, 0)

        @pl.when(m > 0)
        def _():
            halo_up(k).wait_recv()

        @pl.when(m < n_mesh - 1)
        def _():
            halo_down(k).wait_recv()

        advance(k, 0)
        advance(k, block_count - 1)
        if k + 1 < SECTIONS:
            halo_start(k + 1)
    state = states[SECTIONS]

    def sum_over(level):
        width = 2**level
        n = n_mesh * width
        count = min(n, pieces)
        depth = modes // count
        base = p // width * width
        rank = m * width + (p - base)

        def device(t):
            return (t // width, base + lax.rem(t, width))

        def scatter(s, carry):
            t = lax.rem(rank + s, n)
            at = pl.ds(pl.multiple_of(lax.rem(t, count) * depth, depth), depth)
            pltpu.make_async_remote_copy(
                partial[level].at[at], slots[level].at[s - 1], sum_send.at[level], sum_recv.at[level],
                device_id=device(t), device_id_type=MESH).start()
            return carry

        lax.fori_loop(1, n, scatter, 0)
        piece = lax.rem(rank, count)
        own = pl.ds(pl.multiple_of(piece * depth, depth), depth)
        wait_bytes(slots[level], sum_recv.at[level])
        if n <= 64:
            total = partial[level][own, :] + jnp.sum(slots[level][...], 0)
        else:
            total = partial[level][own, :] + lax.fori_loop(
                0, n - 1, lambda i, a: a + slots[level][i], jnp.zeros((depth, modes), F32))
        grams[level][own, :] = total

        def spread(s, carry):
            t = rank - piece + lax.rem(piece + s, count)
            pltpu.make_async_remote_copy(
                grams[level].at[own], grams[level].at[own], all_send.at[level], all_recv.at[level],
                device_id=device(t), device_id_type=MESH).start()
            return carry

        lax.fori_loop(1, count, spread, 0)
        wait_bytes(grams[level].at[pl.ds(0, (count - 1) * depth)], all_recv.at[level])
        return grams[level][...]

    chunk = 512

    def merge_copy(level):
        half = total_rows // 2 ** (level + 1)
        keep = p // 2**level % 2
        if level == 0:
            source = state.at[pl.ds(pl.multiple_of(block + (1 - keep) * half, 16), half)]
        else:
            source = halves[level - 1].at[pl.ds(pl.multiple_of((1 - keep) * half, 16), half)]
        return pltpu.make_async_remote_copy(
            source, partner_rows[level], merge_send.at[level], merge_recv.at[level],
            device_id=(m, p + (1 - 2 * keep) * 2**level), device_id_type=MESH)

    def factor_copy(level):
        keep = p // 2**level % 2
        return pltpu.make_async_remote_copy(
            factors[level], partner_factors[level], factor_send.at[level], factor_recv.at[level],
            device_id=(m, p + (1 - 2 * keep) * 2**level), device_id_type=MESH)

    merge_copy(0).start()
    gram = jnp.zeros((modes, modes), F32)
    for i in range(total_rows // chunk):
        part = state[pl.ds(block + i * chunk, chunk), :]
        gram += cross(part, part)
    partial[0][...] = gram
    factors[0][...] = unit_inverse(sum_over(0)).astype(BF16)

    for level in range(levels):
        half = total_rows // 2 ** (level + 1)
        keep = p // 2**level % 2
        step = min(half, chunk)
        steps = range(half // step)
        factor_copy(level).start()
        mine = sketch_ref[pl.ds(pl.multiple_of(keep * modes, modes), modes), :]
        theirs = sketch_ref[pl.ds(pl.multiple_of((1 - keep) * modes, modes), modes), :]
        weights = jnp.concatenate([mine, theirs], 0)

        def basis_of(pair, factor):
            if level == 0:
                return dot_turned(pair, factor).astype(BF16)
            high = factor[:, :modes]
            total = dot_turned(pair, jnp.concatenate([high, high], 1)) + dot_turned(pair[:, :modes], factor[:, modes:])
            return total.astype(BF16)

        factor = factors[level][...]
        kept = []
        for i in steps:
            at = keep * half + i * step
            if level == 0:
                pair = state[pl.ds(pl.multiple_of(at + block, 16), step), :]
            else:
                pair = halves[level - 1][pl.ds(pl.multiple_of(at, 16), step), :]
            kept.append(basis_of(pair, factor))
        merge_copy(level).wait_recv()
        factor_copy(level).wait_recv()
        factor = partner_factors[level][...]
        gram = jnp.zeros((modes, 2 * modes), F32)
        for i in steps:
            other = basis_of(partner_rows[level][pl.ds(i * step, step), :], factor)
            high, low = split_two(dot(jnp.concatenate([kept[i], other], 1), weights))
            pair = jnp.concatenate([high, low], 1)
            halves[level][pl.ds(i * step, step), :] = pair
            gram += cross(high, pair)
        if level + 1 < levels:
            merge_copy(level + 1).start()
        partial[level + 1][...] = gram[:, :modes] + gram[:, modes:] + gram[:, modes:].T
        high, low = split_two(unit_inverse(sum_over(level + 1)))
        if level + 1 < levels:
            factors[level + 1][...] = jnp.concatenate([high, low], 1)

    share = modes // n_param
    rows = total_rows // n_param
    step = min(rows, chunk)
    twice = jnp.concatenate([high, high], 1)
    for i in range(rows // step):
        pair = halves[levels - 1][pl.ds(i * step, step), :]
        turned[:, pl.ds(i * step, step)] = (dot_turned(twice, pair) + dot_turned(low, pair[:, :modes])).astype(BF16)
    offset = 0
    for level in range(levels):
        offset = offset + p // 2**level % 2 * (total_rows // 2 ** (level + 1))
    place = pl.ds(pl.multiple_of(offset, 128), rows)

    def deliver(s, carry):
        t = lax.rem(p + s, n_param)
        pltpu.make_async_remote_copy(
            turned.at[pl.ds(pl.multiple_of(t * share, 16), share)], result.at[:, place], out_send.at[0], out_recv.at[0],
            device_id=(m, t), device_id_type=MESH).start()
        return carry

    lax.fori_loop(1, n_param, deliver, 0)
    result[:, place] = turned[pl.ds(pl.multiple_of(p * share, 16), share), :]
    others = result.at[:, pl.ds(0, (n_param - 1) * rows)]
    wait_bytes(others, out_recv.at[0])
    out_ref[...] = result[...]

    for k in range(SECTIONS):
        @pl.when(m < n_mesh - 1)
        def _():
            halo_up(k).wait_send()

        @pl.when(m > 0)
        def _():
            halo_down(k).wait_send()
    for level in range(levels):
        merge_copy(level).wait_send()
        factor_copy(level).wait_send()
    for level in range(levels + 1):
        count = min(n_mesh * 2**level, pieces)
        wait_bytes(slots[level], sum_send.at[level])
        wait_bytes(grams[level].at[pl.ds(0, (count - 1) * (modes // count))], all_send.at[level])
    wait_bytes(others, out_send.at[0])


def solution(mesh):
    n_mesh, n_param = mesh.shape["mesh"], mesh.shape["param"]
    levels = n_param.bit_length() - 1

    def on_device(snapshots, coupling, reaction_rate, sketch):
        rows, modes = snapshots.shape
        block = coupling.shape[2]
        pieces = modes // 8
        square = pltpu.VMEM((modes, modes), F32)
        slots = []
        for level in range(levels + 1):
            n = n_mesh * 2**level
            slots.append(pltpu.VMEM((n - 1, modes // min(n, pieces), modes), F32))
        dma = lambda k: pltpu.SemaphoreType.DMA((k,))
        share = modes // n_param
        widths = [modes] + [2 * modes] * (levels - 1)
        scratch = [
            pltpu.VMEM(coupling.shape, BF16),
            pltpu.VMEM((1, modes), F32),
            pltpu.VMEM(sketch.shape, BF16),
            pltpu.VMEM((modes, rows // n_param), BF16),
            pltpu.VMEM((share, rows), BF16),
        ]
        scratch += [pltpu.VMEM((rows + 2 * block, modes), BF16)] * (SECTIONS + 1)
        scratch += [pltpu.VMEM((rows >> (k + 1), widths[k]), BF16) for k in range(levels)]
        scratch += [pltpu.VMEM((modes, widths[k]), BF16) for k in range(levels)] * 2
        scratch += [pltpu.VMEM((rows >> (k + 1), 2 * modes), BF16) for k in range(levels)]
        scratch += [square] * (levels + 1) + slots + [square] * (levels + 1)
        scratch += [dma(4), dma(2 * SECTIONS), dma(2 * SECTIONS)] + [dma(levels)] * 4
        scratch += [dma(levels + 1)] * 4 + [dma(1), dma(1)]
        vmem = pl.BlockSpec(memory_space=pltpu.VMEM)
        anywhere = pl.BlockSpec(memory_space=pltpu.HBM)
        return pl.pallas_call(
            functools.partial(kernel, (n_mesh, n_param, levels, pieces)),
            out_shape=jax.ShapeDtypeStruct((share, rows), BF16),
            in_specs=[anywhere] * 4,
            out_specs=vmem,
            scratch_shapes=scratch,
            compiler_params=pltpu.CompilerParams(
                collective_id=0, has_side_effects=True, vmem_limit_bytes=63 * 1024 * 1024
            ),
        )(snapshots, coupling, reaction_rate.reshape(1, modes), sketch).T

    return jax.shard_map(
        on_device,
        mesh=mesh,
        in_specs=(P("mesh", "param"), P("mesh", None, None, None), P("param"), P()),
        out_specs=P("mesh", "param"),
        check_vma=False,
    )
```

```python
import functools

import jax
import jax.numpy as jnp
from jax import lax
from jax.experimental import pallas as pl
from jax.experimental.pallas import tpu as pltpu
from jax.sharding import PartitionSpec as P

SECTIONS = 3
MESH = pl.DeviceIdType.MESH
F32 = jnp.float32
BF16 = jnp.bfloat16


def split_two(x):
    high = x.astype(BF16)
    return high, (x - high.astype(F32)).astype(BF16)


def split_three(x):
    high = x.astype(BF16).astype(F32)
    middle = (x - high).astype(BF16).astype(F32)
    return high, middle, x - high - middle


def reciprocal(x):
    guess = pl.reciprocal(x, approx=True)
    return guess * (2.0 - x * guess)


def unit_inverse(gram):
    size = gram.shape[0]
    count = size // 8
    tile = (8, size)
    rows = [gram[8 * q : 8 * q + 8, :] for q in range(count)]
    lane = lax.broadcasted_iota(jnp.int32, tile, 1)
    sub = lax.broadcasted_iota(jnp.int32, tile, 0)

    def stacked(parts):
        whole = parts[7]
        for i in range(7):
            whole = jnp.where(sub == i, parts[i], whole)
        return whole

    for p in range(count):
        first = 8 * p
        inside = (lane >= first) & (lane < first + 8)
        corner = [jnp.broadcast_to(rows[p][:, first + j : first + j + 1], tile) for j in range(8)]
        entry = [[jnp.broadcast_to(corner[j][i : i + 1, :], tile) if j >= i else None for j in range(8)] for i in range(8)]
        start = jnp.where(inside, jnp.where(lane - first == sub, 1.0, 0.0), rows[p])
        line = [jnp.broadcast_to(start[i : i + 1, :], tile) for i in range(8)]
        later = [None] * (p + 1) + [jnp.where(inside, 0.0, rows[q]) for q in range(p + 1, count)]
        if p + 1 < count:
            column = [jnp.broadcast_to(rows[p + 1][:, first + j : first + j + 1], tile) for j in range(8)]
        inverse = []
        for i in range(8):
            inverse.append(reciprocal(entry[i][i]))
            for r in range(i + 1, 8):
                scale = entry[i][r] * inverse[i]
                for j in range(r, 8):
                    entry[r][j] = entry[r][j] - scale * entry[i][j]
                line[r] = line[r] - scale * line[i]
            if p + 1 < count:
                scale = column[i] * inverse[i]
                for j in range(i + 1, 8):
                    column[j] = column[j] - scale * entry[i][j]
                later[p + 1] = later[p + 1] - scale * line[i]
        if p + 2 < count:
            left = split_three(stacked([line[i] * inverse[i] for i in range(8)]))
            right = split_three(stacked(line))
            terms = ((0, 0), (0, 1), (1, 0), (0, 2), (2, 0), (1, 1))
            change = cross(
                jnp.concatenate([left[i] for i, _ in terms], 0).astype(BF16),
                jnp.concatenate([right[j] for _, j in terms], 0).astype(BF16))
            for q in range(p + 2, count):
                later[q] = later[q] - change[8 * q : 8 * q + 8, :]
        rows[p] = stacked(line)
        rows[p + 1 :] = later[p + 1 :]
    full = jnp.concatenate(rows, 0)
    row = lax.broadcasted_iota(jnp.int32, (size, size), 0)
    column = lax.broadcasted_iota(jnp.int32, (size, size), 1)
    return jnp.where(column <= row, full, 0.0)


def cross(a, b):
    return lax.dot_general(a, b, (((0,), (0,)), ((), ())), preferred_element_type=F32)


def dot(a, b):
    return jnp.dot(a, b, preferred_element_type=F32)


def dot_turned(a, b):
    return lax.dot_general(a, b, (((1,), (1,)), ((), ())), preferred_element_type=F32)


def wait_bytes(ref, sem):
    pltpu.make_async_copy(ref, ref, sem).wait()


def kernel(plan, snap_ref, coup_ref, rate_hbm, sketch_hbm, out_ref, *scratch):
    n_mesh, n_param, levels, pieces = plan
    scratch = list(scratch)
    take = lambda k: [scratch.pop(0) for _ in range(k)]
    coup, rate_ref, sketch_ref, turned, result = take(5)
    states = take(SECTIONS + 1)
    partner_rows = take(levels)
    factors = take(levels)
    partner_factors = take(levels)
    halves = take(levels)
    partial = take(levels + 1)
    slots = take(levels + 1)
    grams = take(levels + 1)
    load_sem, halo_send, halo_recv, merge_send, merge_recv, factor_send, factor_recv, sum_send, sum_recv, all_send, all_recv, out_send, out_recv = take(13)

    m = lax.axis_index("mesh")
    p = lax.axis_index("param")
    total_rows, modes = snap_ref.shape
    block_count, _, block, _ = coup_ref.shape

    load_state = pltpu.make_async_copy(snap_ref, states[0].at[pl.ds(block, total_rows)], load_sem.at[0])
    load_coup = pltpu.make_async_copy(coup_ref, coup, load_sem.at[1])
    load_rate = pltpu.make_async_copy(rate_hbm, rate_ref, load_sem.at[2])
    load_sketch = pltpu.make_async_copy(sketch_hbm, sketch_ref, load_sem.at[3])
    load_state.start()
    load_coup.start()
    load_rate.start()
    load_sketch.start()

    n_all = n_mesh * n_param
    me = m * n_param + p
    barrier = pltpu.get_barrier_semaphore()

    def greet(s, carry):
        t = lax.rem(me + s, n_all)
        pl.semaphore_signal(barrier, inc=1, device_id=(t // n_param, lax.rem(t, n_param)), device_id_type=MESH)
        return carry

    lax.fori_loop(1, n_all, greet, 0)
    for k in range(SECTIONS):
        @pl.when(m == 0)
        def _():
            states[k][pl.ds(0, block), :] = jnp.zeros((block, modes), BF16)

        @pl.when(m == n_mesh - 1)
        def _():
            states[k][pl.ds(block + total_rows, block), :] = jnp.zeros((block, modes), BF16)
    load_state.wait()
    pl.semaphore_wait(barrier, n_all - 1)

    def halo_up(k):
        return pltpu.make_async_remote_copy(
            states[k].at[pl.ds(total_rows, block)], states[k].at[pl.ds(0, block)],
            halo_send.at[2 * k], halo_recv.at[2 * k], device_id=(m + 1, p), device_id_type=MESH)

    def halo_down(k):
        return pltpu.make_async_remote_copy(
            states[k].at[pl.ds(block, block)], states[k].at[pl.ds(block + total_rows, block)],
            halo_send.at[2 * k + 1], halo_recv.at[2 * k + 1], device_id=(m - 1, p), device_id_type=MESH)

    def halo_start(k):
        @pl.when(m < n_mesh - 1)
        def _():
            halo_up(k).start()

        @pl.when(m > 0)
        def _():
            halo_down(k).start()

    halo_start(0)
    load_rate.wait()
    load_sketch.wait()
    load_coup.wait()
    rate = rate_ref[...]

    def advance(k, b):
        c = coup.at[b]
        operator = jnp.concatenate([c[1], c[0], c[2]], 1)
        start = pl.multiple_of(b * block, block)
        mixed = dot(operator, states[k][pl.ds(start, 3 * block), :])
        at = pl.ds(pl.multiple_of(start + block, block), block)
        current = states[k][at, :].astype(F32)
        states[k + 1][at, :] = ((0.5 * current + 0.5 * mixed) * reciprocal(1.0 + rate * current * current)).astype(BF16)

    inner = block_count - 2
    group = max(g for g in range(1, 11) if inner % g == 0)
    for k in range(SECTIONS):
        def some(i, carry, k=k):
            for j in range(group):
                advance(k, 1 + i * group + j)
            return carry

        lax.fori_loop(0, inner // group, some, 0)

        @pl.when(m > 0)
        def _():
            halo_up(k).wait_recv()

        @pl.when(m < n_mesh - 1)
        def _():
            halo_down(k).wait_recv()

        advance(k, 0)
        advance(k, block_count - 1)
        if k + 1 < SECTIONS:
            halo_start(k + 1)
    state = states[SECTIONS]

    def sum_over(level):
        width = 2**level
        n = n_mesh * width
        count = min(n, pieces)
        depth = modes // count
        base = p // width * width
        rank = m * width + (p - base)

        def device(t):
            return (t // width, base + lax.rem(t, width))

        def scatter(s, carry):
            t = lax.rem(rank + s, n)
            at = pl.ds(pl.multiple_of(lax.rem(t, count) * depth, depth), depth)
            pltpu.make_async_remote_copy(
                partial[level].at[at], slots[level].at[s - 1], sum_send.at[level], sum_recv.at[level],
                device_id=device(t), device_id_type=MESH).start()
            return carry

        lax.fori_loop(1, n, scatter, 0)
        piece = lax.rem(rank, count)
        own = pl.ds(pl.multiple_of(piece * depth, depth), depth)
        wait_bytes(slots[level], sum_recv.at[level])
        if n <= 64:
            total = partial[level][own, :] + jnp.sum(slots[level][...], 0)
        else:
            total = partial[level][own, :] + lax.fori_loop(
                0, n - 1, lambda i, a: a + slots[level][i], jnp.zeros((depth, modes), F32))
        grams[level][own, :] = total

        def spread(s, carry):
            t = rank - piece + lax.rem(piece + s, count)
            pltpu.make_async_remote_copy(
                grams[level].at[own], grams[level].at[own], all_send.at[level], all_recv.at[level],
                device_id=device(t), device_id_type=MESH).start()
            return carry

        lax.fori_loop(1, count, spread, 0)
        wait_bytes(grams[level].at[pl.ds(0, (count - 1) * depth)], all_recv.at[level])
        return grams[level][...]

    chunk = 512

    def merge_copy(level):
        half = total_rows // 2 ** (level + 1)
        keep = p // 2**level % 2
        if level == 0:
            source = state.at[pl.ds(pl.multiple_of(block + (1 - keep) * half, 16), half)]
        else:
            source = halves[level - 1].at[pl.ds(pl.multiple_of((1 - keep) * half, 16), half)]
        return pltpu.make_async_remote_copy(
            source, partner_rows[level], merge_send.at[level], merge_recv.at[level],
            device_id=(m, p + (1 - 2 * keep) * 2**level), device_id_type=MESH)

    def factor_copy(level):
        keep = p // 2**level % 2
        return pltpu.make_async_remote_copy(
            factors[level], partner_factors[level], factor_send.at[level], factor_recv.at[level],
            device_id=(m, p + (1 - 2 * keep) * 2**level), device_id_type=MESH)

    merge_copy(0).start()
    gram = jnp.zeros((modes, modes), F32)
    for i in range(total_rows // chunk):
        part = state[pl.ds(block + i * chunk, chunk), :]
        gram += cross(part, part)
    partial[0][...] = gram
    factors[0][...] = unit_inverse(sum_over(0)).astype(BF16)

    for level in range(levels):
        half = total_rows // 2 ** (level + 1)
        keep = p // 2**level % 2
        step = min(half, chunk)
        steps = range(half // step)
        factor_copy(level).start()
        mine = sketch_ref[pl.ds(pl.multiple_of(keep * modes, modes), modes), :]
        theirs = sketch_ref[pl.ds(pl.multiple_of((1 - keep) * modes, modes), modes), :]
        weights = jnp.concatenate([mine, theirs], 0)

        def basis_of(pair, factor):
            if level == 0:
                return dot_turned(pair, factor).astype(BF16)
            high = factor[:, :modes]
            total = dot_turned(pair, jnp.concatenate([high, high], 1)) + dot_turned(pair[:, :modes], factor[:, modes:])
            return total.astype(BF16)

        factor = factors[level][...]
        kept = []
        for i in steps:
            at = keep * half + i * step
            if level == 0:
                pair = state[pl.ds(pl.multiple_of(at + block, 16), step), :]
            else:
                pair = halves[level - 1][pl.ds(pl.multiple_of(at, 16), step), :]
            kept.append(basis_of(pair, factor))
        merge_copy(level).wait_recv()
        factor_copy(level).wait_recv()
        factor = partner_factors[level][...]
        gram = jnp.zeros((modes, 2 * modes), F32)
        for i in steps:
            other = basis_of(partner_rows[level][pl.ds(i * step, step), :], factor)
            high, low = split_two(dot(jnp.concatenate([kept[i], other], 1), weights))
            pair = jnp.concatenate([high, low], 1)
            halves[level][pl.ds(i * step, step), :] = pair
            gram += cross(high, pair)
        if level + 1 < levels:
            merge_copy(level + 1).start()
        partial[level + 1][...] = gram[:, :modes] + gram[:, modes:] + gram[:, modes:].T
        high, low = split_two(unit_inverse(sum_over(level + 1)))
        if level + 1 < levels:
            factors[level + 1][...] = jnp.concatenate([high, low], 1)

    share = modes // n_param
    rows = total_rows // n_param
    step = min(rows, chunk)
    twice = jnp.concatenate([high, high], 1)
    for i in range(rows // step):
        pair = halves[levels - 1][pl.ds(i * step, step), :]
        turned[:, pl.ds(i * step, step)] = (dot_turned(twice, pair) + dot_turned(low, pair[:, :modes])).astype(BF16)
    offset = 0
    for level in range(levels):
        offset = offset + p // 2**level % 2 * (total_rows // 2 ** (level + 1))
    place = pl.ds(pl.multiple_of(offset, 128), rows)

    def deliver(s, carry):
        t = lax.rem(p + s, n_param)
        pltpu.make_async_remote_copy(
            turned.at[pl.ds(pl.multiple_of(t * share, 16), share)], result.at[:, place], out_send.at[0], out_recv.at[0],
            device_id=(m, t), device_id_type=MESH).start()
        return carry

    lax.fori_loop(1, n_param, deliver, 0)
    result[:, place] = turned[pl.ds(pl.multiple_of(p * share, 16), share), :]
    others = result.at[:, pl.ds(0, (n_param - 1) * rows)]
    wait_bytes(others, out_recv.at[0])
    out_ref[...] = result[...]

    for k in range(SECTIONS):
        @pl.when(m < n_mesh - 1)
        def _():
            halo_up(k).wait_send()

        @pl.when(m > 0)
        def _():
            halo_down(k).wait_send()
    for level in range(levels):
        merge_copy(level).wait_send()
        factor_copy(level).wait_send()
    for level in range(levels + 1):
        count = min(n_mesh * 2**level, pieces)
        wait_bytes(slots[level], sum_send.at[level])
        wait_bytes(grams[level].at[pl.ds(0, (count - 1) * (modes // count))], all_send.at[level])
    wait_bytes(others, out_send.at[0])


def solution(mesh):
    n_mesh, n_param = mesh.shape["mesh"], mesh.shape["param"]
    levels = n_param.bit_length() - 1

    def on_device(snapshots, coupling, reaction_rate, sketch):
        rows, modes = snapshots.shape
        block = coupling.shape[2]
        pieces = modes // 8
        square = pltpu.VMEM((modes, modes), F32)
        slots = []
        for level in range(levels + 1):
            n = n_mesh * 2**level
            slots.append(pltpu.VMEM((n - 1, modes // min(n, pieces), modes), F32))
        dma = lambda k: pltpu.SemaphoreType.DMA((k,))
        share = modes // n_param
        widths = [modes] + [2 * modes] * (levels - 1)
        scratch = [
            pltpu.VMEM(coupling.shape, BF16),
            pltpu.VMEM((1, modes), F32),
            pltpu.VMEM(sketch.shape, BF16),
            pltpu.VMEM((modes, rows // n_param), BF16),
            pltpu.VMEM((share, rows), BF16),
        ]
        scratch += [pltpu.VMEM((rows + 2 * block, modes), BF16)] * (SECTIONS + 1)
        scratch += [pltpu.VMEM((rows >> (k + 1), widths[k]), BF16) for k in range(levels)]
        scratch += [pltpu.VMEM((modes, widths[k]), BF16) for k in range(levels)] * 2
        scratch += [pltpu.VMEM((rows >> (k + 1), 2 * modes), BF16) for k in range(levels)]
        scratch += [square] * (levels + 1) + slots + [square] * (levels + 1)
        scratch += [dma(4), dma(2 * SECTIONS), dma(2 * SECTIONS)] + [dma(levels)] * 4
        scratch += [dma(levels + 1)] * 4 + [dma(1), dma(1)]
        vmem = pl.BlockSpec(memory_space=pltpu.VMEM)
        anywhere = pl.BlockSpec(memory_space=pltpu.HBM)
        return pl.pallas_call(
            functools.partial(kernel, (n_mesh, n_param, levels, pieces)),
            out_shape=jax.ShapeDtypeStruct((share, rows), BF16),
            in_specs=[anywhere] * 4,
            out_specs=vmem,
            scratch_shapes=scratch,
            compiler_params=pltpu.CompilerParams(
                collective_id=0, has_side_effects=True, vmem_limit_bytes=63 * 1024 * 1024
            ),
        )(snapshots, coupling, reaction_rate.reshape(1, modes), sketch).T

    return jax.shard_map(
        on_device,
        mesh=mesh,
        in_specs=(P("mesh", "param"), P("mesh", None, None, None), P("param"), P()),
        out_specs=P("mesh", "param"),
        check_vma=False,
    )
```
